256 devices in a mesh: ma: 32 (over z, y), freq: 8 (over x, core).
Axes of the slice: x: 4, y: 4, z: 8, core: 2. Of those that a mesh axis runs over, the one named last changes fastest.
Arguments:
- visibilities: bfloat16 [512, 32, 4, 512], P('ma', 'freq'), may hold values from -6 to 6
- transfer: bfloat16 [32, 64, 512, 1024], P('freq', 'ma'), may hold values from -1 to 1, as said below
- noise_weight: float32 [32, 512], P('freq'), may hold values from 1 to 12, as said below
- freq_prior: float32 [32, 32], P('freq'), may hold values from -1 to 5, as said below
Outputs:
- sky_map: float32 [32, 64, 4, 1024], P('freq', 'ma')
- residual: float32 [32, 64, 4, 1024], P('freq', 'ma')
- direction: float32 [32, 64, 4, 1024], P('freq', 'ma')
The draws below stay inside these ranges and needn't reach their ends.
Inputs may be any that keep to these rules, and one draw needn't show every extreme that they name: Real transfer blocks of the m-modes in the window. `noise_weight`: positive weights. `freq_prior`: symmetric positive definite.
All inputs are finite; a program needn't handle non-finite values.
Results may differ from the reference program's by a relative error of at most 0.0056.
Values may be sent and summed in bfloat16 or wider, within the bound.
A program may use at most 64 MiB of HBM per device.

```python
import math
import jax
import jax.numpy as jnp
from jax import lax

NB = 512
NS = 1024
SIMS = 4
M = 64
F = 32
NT = 512


def draw_transfer(key, part):
    key = jax.random.fold_in(key, 1)
    extent = (F, M, NB, NS)
    raw_values = jnp.clip(jax.random.normal(key, extent, jnp.float32), -4.0, 4.0)
    falloff = jnp.exp(-math.log(3.0) * jnp.arange(M, dtype=jnp.float32) / max(M - 1, 1))
    return (raw_values * falloff[None, :, None, None] * (1.6 / math.sqrt(NS))).astype(jnp.bfloat16)


def draw_noise_weight(key, part):
    key = jax.random.fold_in(key, 2)
    rising = jnp.exp(math.log(3.0) * jnp.arange(F, dtype=jnp.float32) / max(F - 1, 1))
    spread = jnp.exp(jax.random.uniform(key, (F, NB), jnp.float32, 0.0, math.log(4.0)))
    return rising[:, None] * spread


def draw_freq_prior(key, part):
    key = jax.random.fold_in(key, 3)
    key_off, key_diag = jax.random.split(key)
    raw_values = jax.random.uniform(key_off, (F, F), jnp.float32, -1.0, 1.0)
    off_diagonal = (raw_values + raw_values.T) * (1.5 / F)
    diagonal = 3.2 + 1.5 * jax.random.uniform(key_diag, (F,), jnp.float32)
    positions = jnp.arange(F, dtype=jnp.int32)
    same_place = positions[:, None] == positions[None, :]
    return jnp.where(same_place, diagonal[:, None], off_diagonal)


def block_levels(rng, shape, shards, low, high):
    gain = 1.0
    for dim, parts in shards:
        heights = jax.random.uniform(jax.random.fold_in(jax.random.fold_in(rng, 6), dim), (parts,), jnp.float32, low / len(shards), high / len(shards))
        gain = gain * jnp.repeat(jnp.exp(heights), shape[dim] // parts).reshape((-1,) + (1,) * (len(shape) - 1 - dim))
    return gain


def centred(key, dims, scale, bound, pieces=(), held_as=jnp.bfloat16):
    values = scale * jax.random.normal(key, dims, jnp.float32)
    if pieces:
        values = values * block_levels(key, dims, pieces, -0.22, 0.18)
    return jnp.clip(values, -bound, bound).astype(held_as)


def setup_inputs(seed: int = 0) -> dict:
    splits = jax.random.split(jax.random.key(seed), 5)
    return {
        "visibilities": centred(splits[0], (NT, F, SIMS, NB), 1.0, 6.0, ((0, 32), (1, 8))),
        "transfer": draw_transfer(jax.random.fold_in(splits[4], 71), 0),
        "noise_weight": draw_noise_weight(jax.random.fold_in(splits[4], 71), 0),
        "freq_prior": draw_freq_prior(jax.random.fold_in(splits[4], 71), 0),
    }


def harmonic_lookup(lowest_harmonic_index, harmonic_number, leading_epoch, epoch_number, whole_epoch_grid):
    harmonic_slot = lowest_harmonic_index + jnp.arange(harmonic_number, dtype=jnp.int32)
    observing_epochs = leading_epoch + jnp.arange(epoch_number, dtype=jnp.int32)
    rotation_argument = harmonic_slot[:, None] * observing_epochs[None, :] % whole_epoch_grid
    rotation_radians = rotation_argument.astype(jnp.float32) * (2.0 * math.pi / whole_epoch_grid)
    return ((jnp.cos(rotation_radians) + jnp.sin(rotation_radians)) * (1.0 / math.sqrt(whole_epoch_grid))).astype(jnp.bfloat16)

def reference(visibilities, transfer, noise_weight, freq_prior):
    highest = lax.Precision.HIGHEST
    cas_values = lax.optimization_barrier(harmonic_lookup(0, M, 0, NT, NT))
    visibility_modes = jnp.einsum('mt,tfkb->mfkb', cas_values.astype(jnp.float32), visibilities.astype(jnp.float32), precision=highest)
    weighted = lax.optimization_barrier((noise_weight[None, :, None, :] * visibility_modes).astype(jnp.bfloat16))
    weighted = jnp.transpose(weighted, (1, 0, 2, 3)).reshape(F * M, SIMS, NB)
    blocks = transfer.reshape(F * M, NB, NS)

    def project_back(operands):
        single_block, vectors = operands
        return jnp.einsum('bs,kb->ks', single_block.astype(jnp.float32), vectors.astype(jnp.float32), precision=highest)
    right_side = lax.map(project_back, (blocks, weighted)).reshape(F, M, SIMS, NS)
    right_low = lax.optimization_barrier(right_side.astype(jnp.bfloat16))
    block_weights = jnp.repeat(noise_weight, M, axis=0)

    def normal_apply(operands):
        single_block, vectors, scales = operands
        widened = single_block.astype(jnp.float32)
        observed = jnp.einsum('bs,ks->kb', widened, vectors.astype(jnp.float32), precision=highest)
        scaled = lax.optimization_barrier((scales[None, :] * observed).astype(jnp.bfloat16))
        return jnp.einsum('bs,kb->ks', widened, scaled.astype(jnp.float32), precision=highest)
    adjoint = lax.map(normal_apply, (blocks, right_low.reshape(F * M, SIMS, NS), block_weights)).reshape(F, M, SIMS, NS)
    coupled = jnp.einsum('fg,gmks->fmks', freq_prior, right_side, precision=highest)
    applied = adjoint + coupled
    norm_now = lax.optimization_barrier(jnp.sum(right_side * right_side, axis=(0, 1, 3)))
    curvature = lax.optimization_barrier(jnp.sum(right_side * applied, axis=(0, 1, 3)))
    step_size = (norm_now / curvature)[None, None, :, None]
    sky_map = step_size * right_side
    residual = right_side - step_size * applied
    norm_next = lax.optimization_barrier(jnp.sum(residual * residual, axis=(0, 1, 3)))
    direction = residual + (norm_next / norm_now)[None, None, :, None] * right_side
    return (sky_map, residual, direction)
```

```python
import math

import jax
import jax.numpy as jnp
import numpy as np
from jax import lax
from jax.experimental import pallas as pl
from jax.experimental.pallas import tpu as pltpu
from jax.sharding import PartitionSpec as P

NZ, NY, NX, NC = 8, 4, 4, 2
NF, NM, NB, NS, SIMS, NT, TL = 4, 2, 512, 1024, 4, 512, 16
ROWS = NM * SIMS
F32, BF16 = jnp.float32, jnp.bfloat16
HIGH = lax.Precision.HIGHEST


def cas_table():
    m = np.arange(64)
    t = np.arange(NT)
    arg = (m[:, None] * t[None, :]) % NT
    ang = arg.astype(np.float32) * np.float32(2.0 * math.pi / NT)
    cas = (np.cos(ang) + np.sin(ang)) * np.float32(1.0 / math.sqrt(NT))
    cas = cas.reshape(64, NZ, 64).transpose(1, 0, 2)
    eye = np.eye(SIMS, dtype=np.float32)
    full = cas[:, :, None, :, None] * eye[None, None, :, None, :]
    return full.reshape(NZ, 256, 256).astype(jnp.bfloat16)


def dot(a, b, **kw):
    return jnp.dot(a, b, preferred_element_type=F32, **kw)


def dot_t(a, b):
    return lax.dot_general(a, b, (((1,), (1,)), ((), ())), preferred_element_type=F32)


def kernel(vis, transfer, weight, prior, cas, right_out, applied_out, coef_out,
           tv, casv, vbuf, pbuf, rbuf, right, adj, rall, sib_out, sib_in, prior_sib, dsend, d1, d2,
           tsem, lsem, ps, a1s, a1r, a2s, a2r, cs, cr, ss, sr, d1s, d1r, d2s, d2r):
    ma = lax.axis_index("ma")
    fq = lax.axis_index("freq")
    z, y = ma // NY, ma % NY
    x, c = fq // NC, fq % NC

    def ma_peer(dz, dy):
        return lax.rem(z + dz, NZ) * NY + lax.rem(y + dy, NY)

    def fq_peer(dx, dc):
        return lax.rem(x + dx, NX) * NC + lax.rem(c + dc, NC)

    ma_offsets = [(dz, dy) for dz in range(NZ) for dy in range(NY) if dz or dy]
    fq_offsets = [(dx, dc) for dx in range(NX) for dc in range(NC) if dx or dc]

    tcopies = [pltpu.make_async_copy(transfer.at[f], tv.at[f], tsem.at[f]) for f in range(NF)]
    cas_copy = pltpu.make_async_copy(cas.at[z], casv, lsem.at[0])
    own_vis = pltpu.make_async_copy(vis.at[y], vbuf.at[y], lsem.at[1])
    cas_copy.start()
    own_vis.start()

    barrier = pltpu.get_barrier_semaphore()
    for dz, dy in ma_offsets:
        pl.semaphore_signal(barrier, 1, device_id={"ma": ma_peer(dz, dy), "freq": fq})
    for dx, dc in fq_offsets:
        pl.semaphore_signal(barrier, 1, device_id={"ma": ma, "freq": fq_peer(dx, dc)})
    pl.semaphore_wait(barrier, len(ma_offsets) + len(fq_offsets))

    a1 = []
    for dy in range(1, NY):
        a1.append(pltpu.make_async_remote_copy(
            vis.at[lax.rem(y + dy, NY)], vbuf.at[y], a1s.at[dy - 1], a1r.at[dy - 1],
            device_id={"ma": ma_peer(0, dy), "freq": fq}))
        a1[-1].start()
    pc = pltpu.make_async_remote_copy(prior, prior_sib, ps.at[0], ps.at[1],
                                      device_id={"ma": ma, "freq": fq_peer(0, 1)})
    pc.start()
    for t in tcopies:
        t.start()

    pc.wait()

    def spread(p):
        i0 = lax.broadcasted_iota(jnp.int32, (NF * ROWS, NF), 0)
        i1 = lax.broadcasted_iota(jnp.int32, (NF * ROWS, NF), 1)
        e1 = (i0 // ROWS == i1).astype(F32)
        j0 = lax.broadcasted_iota(jnp.int32, (32, NX * NF * ROWS), 0)
        j1 = lax.broadcasted_iota(jnp.int32, (32, NX * NF * ROWS), 1)
        g = (j1 // 32) * 8 + c * 4 + (j1 // 8) % 4
        e2 = (j0 == g).astype(F32)
        k0 = lax.broadcasted_iota(jnp.int32, (NF * ROWS, NX * NF * ROWS), 0)
        k1 = lax.broadcasted_iota(jnp.int32, (NF * ROWS, NX * NF * ROWS), 1)
        full = dot(dot(e1, p, precision=HIGH), e2, precision=HIGH)
        return jnp.where(k0 % ROWS == k1 % ROWS, full, 0.0)

    pri = jnp.concatenate([spread(prior[...]), spread(prior_sib[...])], axis=0)
    pri_hi = pri.astype(BF16)
    pri_lo = (pri - pri_hi.astype(F32)).astype(BF16)
    pri_all = jnp.concatenate([pri_hi, pri_lo], axis=0)

    cas_copy.wait()
    own_vis.wait()
    for r in a1:
        r.wait()

    part = dot(casv[...], vbuf[...].reshape(256, NB)).reshape(32, ROWS, NB)
    pbuf[...] = jnp.concatenate([part[:, :, :256], part[:, :, 256:]], axis=1).astype(BF16)
    a2 = []
    for dz, dy in ma_offsets:
        slot = dz * NY + dy - 1
        peer = ma_peer(dz, dy)
        a2.append(pltpu.make_async_remote_copy(
            pbuf.at[peer], rbuf.at[slot], a2s, a2r, device_id={"ma": peer, "freq": fq}))
        a2[-1].start()
    for t in tcopies:
        t.wait()
    rcv = pltpu.make_async_copy(rbuf, rbuf, a2r)
    rcv.wait()

    row = lax.broadcasted_iota(jnp.int32, (ROWS, 1), 0)
    low = row < SIMS

    def both(a, f, form):
        return jnp.where(low, form(a, tv[f, 0]), form(a, tv[f, 1]))

    for dy in range(NY):
        f = lax.rem(y + NY - dy, NY)
        total = None
        for dz in range(NZ):
            slot = dz * NY + dy
            piece = pbuf[ma] if slot == 0 else rbuf[slot - 1]
            piece = piece.astype(F32)
            total = piece if total is None else total + piece
        modes = jnp.concatenate([total[:ROWS], total[ROWS:]], axis=1)
        weighted = (weight[pl.ds(f, 1), :] * modes).astype(BF16)
        right[f] = both(weighted, f, dot)

    rall[x] = right[...].reshape(NF * ROWS, NS).astype(BF16)
    cc = []
    for dx in range(1, NX):
        cc.append(pltpu.make_async_remote_copy(
            rall.at[x], rall.at[x], cs.at[dx - 1], cr.at[dx - 1],
            device_id={"ma": ma, "freq": fq_peer(dx, 0)}))
        cc[-1].start()

    for f in range(NF):
        observed = both(right[f].astype(BF16), f, dot_t)
        scaled = (weight[pl.ds(f, 1), :] * observed).astype(BF16)
        adj[f] = both(scaled, f, dot)

    for r in cc:
        r.wait()
    cp = dot(pri_all, rall[...].reshape(NX * NF * ROWS, NS))
    cp = cp[:64] + cp[64:]
    sib_out[...] = cp[32:].astype(BF16)
    sc = pltpu.make_async_remote_copy(sib_out, sib_in, ss, sr,
                                      device_id={"ma": ma, "freq": fq_peer(0, 1)})
    sc.start()
    part_applied = adj[...].reshape(NF * ROWS, NS) + cp[:32]
    sc.wait()
    applied = (part_applied + sib_in[...].astype(F32)).reshape(NF, ROWS, NS)
    rt = right[...]
    applied_out[...] = applied
    right_out[...] = rt

    def rows(v):
        return jnp.sum(jnp.sum(v, axis=0), axis=1, keepdims=True)

    lane = lax.broadcasted_iota(jnp.int32, (ROWS, 128), 1)
    n, cu, q = rows(rt * rt), rows(rt * applied), rows(applied * applied)
    own = jnp.where(lane == 0, n, jnp.where(lane == 1, cu, jnp.where(lane == 2, q, 0.0)))
    dsend[0] = own
    dd = []
    for i, (dz, dy) in enumerate(ma_offsets):
        dd.append(pltpu.make_async_remote_copy(
            dsend.at[0], d1.at[i], d1s, d1r, device_id={"ma": ma_peer(dz, dy), "freq": fq}))
        dd[-1].start()
    pltpu.make_async_copy(d1, d1, d1r).wait()
    own = own + jnp.sum(d1[...], axis=0)
    dsend[1] = own
    de = []
    for i, (dx, dc) in enumerate(fq_offsets):
        de.append(pltpu.make_async_remote_copy(
            dsend.at[1], d2.at[i], d2s, d2r, device_id={"ma": ma, "freq": fq_peer(dx, dc)}))
        de[-1].start()
    pltpu.make_async_copy(d2, d2, d2r).wait()
    coef_out[...] = own + jnp.sum(d2[...], axis=0)
    for r in a2 + dd + de:
        r.wait_send()


def local(visibilities, transfer, noise_weight, freq_prior):
    vis = visibilities.transpose(1, 0, 2, 3).reshape(NF, TL * SIMS, NB)
    vm = pl.BlockSpec(memory_space=pltpu.VMEM)
    hbm = pl.BlockSpec(memory_space=pl.ANY)
    dma = pltpu.SemaphoreType.DMA
    out = jax.ShapeDtypeStruct((NF, ROWS, NS), F32)
    right, applied, sums = pl.pallas_call(
        kernel,
        out_shape=(out, out, jax.ShapeDtypeStruct((ROWS, 128), F32)),
        in_specs=[hbm, hbm, vm, vm, hbm],
        out_specs=(vm, vm, vm),
        scratch_shapes=[
            pltpu.VMEM((NF, NM, NB, NS), BF16),
            pltpu.VMEM((256, 256), BF16),
            pltpu.VMEM((NY, TL * SIMS, NB), BF16),
            pltpu.VMEM((32, 16, 256), BF16),
            pltpu.VMEM((31, 16, 256), BF16),
            pltpu.VMEM((NF, ROWS, NS), F32),
            pltpu.VMEM((NF, ROWS, NS), F32),
            pltpu.VMEM((NX, NF * ROWS, NS), BF16),
            pltpu.VMEM((NF * ROWS, NS), BF16),
            pltpu.VMEM((NF * ROWS, NS), BF16),
            pltpu.VMEM((NF, 32), F32),
            pltpu.VMEM((2, ROWS, 128), F32),
            pltpu.VMEM((31, ROWS, 128), F32),
            pltpu.VMEM((7, ROWS, 128), F32),
            dma((NF,)), dma((2,)), dma((2,)), dma((3,)), dma((3,)), dma, dma, dma((3,)), dma((3,)),
            dma, dma, dma, dma, dma, dma,
        ],
        compiler_params=pltpu.CompilerParams(
            collective_id=0, has_side_effects=True, vmem_limit_bytes=40 * 1024 * 1024),
    )(vis, transfer, noise_weight, freq_prior, jnp.asarray(cas_table()))
    sums = sums[:SIMS, :3] + sums[SIMS:, :3]
    norm, curve, image = sums[:, 0], sums[:, 1], sums[:, 2]
    step = norm / curve
    ratio = (image / curve) * step - 1.0
    right = right.reshape(NF, NM, SIMS, NS)
    applied = applied.reshape(NF, NM, SIMS, NS)
    step, ratio = step[:, None], ratio[:, None]
    residual = right - step * applied
    return step * right, residual, residual + ratio * right


def solution(mesh):
    return jax.shard_map(
        local,
        mesh=mesh,
        in_specs=(
            P("ma", "freq", None, None),
            P("freq", "ma", None, None),
            P("freq", None),
            P("freq", None),
        ),
        out_specs=(P("freq", "ma", None, None),) * 3,
        check_vma=False,
    )
```

```python
import math

import jax
import jax.numpy as jnp
import numpy as np
from jax import lax
from jax.experimental import pallas as pl
from jax.experimental.pallas import tpu as pltpu
from jax.sharding import PartitionSpec as P

NZ, NY, NX, NC = 8, 4, 4, 2
NFQ = NX * NC
NF, NM, NB, NS, SIMS, NT, TL = 4, 2, 512, 1024, 4, 512, 16
F = NF * NFQ
ROWS = NM * SIMS
OWN = NF * ROWS
LANES = NS // NFQ
HALF = NB // 2
F32, BF16 = jnp.float32, jnp.bfloat16
HIGH = lax.Precision.HIGHEST
MA_OFFSETS = [(dz, dy) for dz in range(NZ) for dy in range(NY) if dz or dy]
FQ_OFFSETS = [(dx, dc) for dx in range(NX) for dc in range(NC) if dx or dc]


def cas_table():
    m = np.arange(64)
    t = np.arange(NT)
    arg = (m[:, None] * t[None, :]) % NT
    ang = arg.astype(np.float32) * np.float32(2.0 * math.pi / NT)
    cas = (np.cos(ang) + np.sin(ang)) * np.float32(1.0 / math.sqrt(NT))
    cas = cas.reshape(64, NZ, 64).transpose(1, 0, 2)
    eye = np.eye(SIMS, dtype=np.float32)
    full = cas[:, :, None, :, None] * eye[None, None, :, None, :]
    return full.reshape(NZ, 256, 256).astype(jnp.bfloat16)


def dot(a, b, **kw):
    return jnp.dot(a, b, preferred_element_type=F32, **kw)


def dot_t(a, b):
    return lax.dot_general(a, b, (((1,), (1,)), ((), ())), preferred_element_type=F32)


def iota(shape, dim):
    return lax.broadcasted_iota(jnp.int32, shape, dim)


def lane_tiles(v):
    v = sum(v[i * ROWS:(i + 1) * ROWS] for i in range(NF))
    return sum(v[:, i * 128:(i + 1) * 128] for i in range(NS // 128))


def kernel(vis, transfer, weight_hbm, prior_hbm, cas, right_out, applied_out, coef_out,
           tv, gram, casv, vbuf, pbuf, rbuf, right, adj, rsl, rin, asl, ain, csl, cin, prior, spread, weight, dsend, d1, d2,
           tsem, lsem, ps, pr, a1s, a1r, a2s, a2r, rs, rr, as_, ar, cs, cr, d1s, d1r, d2s, d2r):
    ma = lax.axis_index("ma")
    fq = lax.axis_index("freq")
    z, y = ma // NY, ma % NY
    x, c = fq // NC, fq % NC

    def ma_peer(dz, dy):
        return lax.rem(z + dz, NZ) * NY + lax.rem(y + dy, NY)

    def fq_peer(dx, dc):
        return lax.rem(x + dx, NX) * NC + lax.rem(c + dc, NC)

    def to_ma(dz, dy):
        return {"ma": ma_peer(dz, dy), "freq": fq}

    def to_fq(dx, dc):
        return {"ma": ma, "freq": fq_peer(dx, dc)}

    tcopies = [pltpu.make_async_copy(transfer.at[f], tv.at[f], tsem.at[f]) for f in range(NF)]
    halves = [pl.ds(h * HALF, HALF) for h in range(2)]
    cas_copy = pltpu.make_async_copy(cas.at[z], casv, lsem.at[0])
    own_vis = [pltpu.make_async_copy(vis.at[:, y, :, halves[h]], vbuf.at[h, y], lsem.at[1 + h]) for h in range(2)]
    own_prior = pltpu.make_async_copy(prior_hbm, prior.at[fq], lsem.at[3])
    own_weight = pltpu.make_async_copy(weight_hbm, weight, lsem.at[4])
    local_copies = [*own_vis, cas_copy, own_prior, own_weight]
    for t in local_copies:
        t.start()

    barrier = pltpu.get_barrier_semaphore()
    for o in MA_OFFSETS:
        pl.semaphore_signal(barrier, 1, device_id=to_ma(*o))
    for o in FQ_OFFSETS:
        pl.semaphore_signal(barrier, 1, device_id=to_fq(*o))
    pl.semaphore_wait(barrier, len(MA_OFFSETS) + len(FQ_OFFSETS))
    pending = []

    def send(src, dst, ssem, rsem, peer):
        copy = pltpu.make_async_remote_copy(src, dst, ssem, rsem, device_id=peer)
        copy.start()
        pending.append(copy)
        return copy

    a1 = [[send(vis.at[:, lax.rem(y + dy, NY), :, halves[h]], vbuf.at[h, y], a1s.at[h, dy - 1], a1r.at[h, dy - 1],
                to_ma(0, dy)) for dy in range(1, NY)] for h in range(2)]
    pcs = [send(prior_hbm, prior.at[fq], ps.at[i], pr.at[i], to_fq(*o)) for i, o in enumerate(FQ_OFFSETS)]
    for t in tcopies:
        t.start()
    cas_copy.wait()

    for h in range(2):
        own_vis[h].wait()
        for r in a1[h]:
            r.wait_recv()
        part = dot(casv[...], vbuf[h].reshape(256, HALF)).reshape(32, ROWS, HALF)
        pbuf[h] = jnp.concatenate([part[:, :, :128], part[:, :, 128:]], axis=1).astype(BF16)
        for dz, dy in MA_OFFSETS:
            send(pbuf.at[h, ma_peer(dz, dy)], rbuf.at[h, dz * NY + dy - 1], a2s, a2r.at[h], to_ma(dz, dy))

    own_prior.wait()
    own_weight.wait()
    for r in pcs:
        r.wait_recv()
    e1 = (iota((F * ROWS, F), 0) // ROWS == iota((F * ROWS, F), 1)).astype(F32)
    e2 = (iota((F, F * ROWS), 0) == iota((F, F * ROWS), 1) // ROWS).astype(F32)
    full = dot(dot(e1, prior[...].reshape(F, F), precision=HIGH), e2, precision=HIGH)
    same = iota((F * ROWS, F * ROWS), 0) % ROWS == iota((F * ROWS, F * ROWS), 1) % ROWS
    full = jnp.where(same, full, 0.0)
    spread[0] = full.astype(BF16)
    spread[1] = (full - full.astype(BF16).astype(F32)).astype(BF16)
    for t in tcopies:
        t.wait()

    @pl.loop(0, NF)
    def _(f):
        for m in range(NM):
            block = tv[f, m]
            gram[f, m] = dot_t(block, block).astype(BF16)

    low = iota((ROWS, 1), 0) < SIMS

    def both(a, ref, f, at=slice(None)):
        return jnp.where(low, dot(a, ref[f, 0, at]), dot(a, ref[f, 1, at]))

    acc, obs = [None] * NY, [None] * NY
    for h in range(2):
        pltpu.make_async_copy(rbuf.at[h], rbuf.at[h], a2r.at[h]).wait()
        for dy in range(NY):
            f = lax.rem(y + NY - dy, NY)
            total = None
            for dz in range(NZ):
                slot = dz * NY + dy
                piece = pbuf[h, ma] if slot == 0 else rbuf[h, slot - 1]
                piece = piece.astype(F32)
                total = piece if total is None else total + piece
            modes = jnp.concatenate([total[:ROWS], total[ROWS:]], axis=1)
            weighted = (weight[pl.ds(f, 1), halves[h]] * modes).astype(BF16)
            out = both(weighted, tv, f, halves[h])
            acc[dy] = out if h == 0 else acc[dy] + out
            out = both(weighted, gram, f, halves[h])
            obs[dy] = out if h == 0 else obs[dy] + out
    for dy in range(NY):
        right[lax.rem(y + NY - dy, NY)] = acc[dy]

    def slices(v, ref):
        v = v.astype(BF16)
        for j in range(NFQ):
            ref[j] = v[:, j * LANES:(j + 1) * LANES]

    rt = right[...].reshape(OWN, NS)
    slices(rt, rsl)
    rc = [send(rsl.at[fq_peer(*o)], rin.at[fq], rs.at[i], rr.at[i], to_fq(*o)) for i, o in enumerate(FQ_OFFSETS)]
    rin[fq] = rsl[fq]

    for dy in range(NY):
        f = lax.rem(y + NY - dy, NY)
        scaled = (weight[pl.ds(f, 1), :] * obs[dy]).astype(BF16)
        adj[f] = both(scaled, tv, f)
    at = adj[...].reshape(OWN, NS)
    slices(at, asl)
    ac = [send(asl.at[fq_peer(*o)], ain.at[fq], as_.at[i], ar.at[i], to_fq(*o)) for i, o in enumerate(FQ_OFFSETS)]
    ain[fq] = asl[fq]

    for r in rc:
        r.wait_recv()
    rall = rin[...].reshape(F * ROWS, LANES)
    coupled = dot(spread[...].reshape(2 * F * ROWS, F * ROWS), rall)
    coupled = coupled[:F * ROWS] + coupled[F * ROWS:]
    csl[...] = coupled.reshape(NFQ, OWN, LANES)
    cc = [send(csl.at[fq_peer(*o)], cin.at[fq], cs.at[i], cr.at[i], to_fq(*o)) for i, o in enumerate(FQ_OFFSETS)]
    cin[fq] = csl[fq]

    def blocks(v):
        return sum(v[i * ROWS:(i + 1) * ROWS] for i in range(F))

    n = lane_tiles(rt * rt)
    cu = lane_tiles(rt * at) + blocks(rall.astype(F32) * coupled)
    q = lane_tiles(at * at)
    for r in ac:
        r.wait_recv()
    q = q + blocks((2.0 * ain[...].reshape(F * ROWS, LANES).astype(F32) + coupled) * coupled)

    row, lane = iota((ROWS, 128), 0), iota((ROWS, 128), 1)

    def put(v, at_lane):
        return jnp.where(lane == row + at_lane, jnp.sum(v, axis=1, keepdims=True), 0.0)

    own = jnp.sum(put(n, 0) + put(cu, ROWS) + put(q, 2 * ROWS), axis=0, keepdims=True)
    dsend[0] = own
    for i, o in enumerate(MA_OFFSETS):
        send(dsend.at[0], d1.at[i], d1s, d1r, to_ma(*o))
    for f in range(NF):
        for m in range(NM):
            right_out[f, m] = right[f, m * SIMS:(m + 1) * SIMS]
    pltpu.make_async_copy(d1, d1, d1r).wait()
    own = own + jnp.sum(d1[...], axis=0)
    dsend[1] = own
    for i, o in enumerate(FQ_OFFSETS):
        send(dsend.at[1], d2.at[i], d2s, d2r, to_fq(*o))
    for r in cc:
        r.wait_recv()
    for f in range(NF):
        coup = jnp.concatenate([cin[j, f * ROWS:(f + 1) * ROWS] for j in range(NFQ)], axis=1)
        applied = adj[f] + coup
        for m in range(NM):
            applied_out[f, m] = applied[m * SIMS:(m + 1) * SIMS]
    pltpu.make_async_copy(d2, d2, d2r).wait()
    own = own + jnp.sum(d2[...], axis=0)

    def take(at_lane):
        inside = (lane >= at_lane) & (lane < at_lane + ROWS) & (lane % SIMS == row % SIMS)
        return jnp.sum(jnp.where(inside, own, 0.0), axis=1, keepdims=True)

    norm, curve, image = take(0), take(ROWS), take(2 * ROWS)
    step = norm / curve
    ratio = (image / curve) * step - 1.0
    coef_out[0] = jnp.broadcast_to(step[:SIMS], (SIMS, 128))
    coef_out[1] = jnp.broadcast_to(ratio[:SIMS], (SIMS, 128))
    for r in pending:
        r.wait_send()


def local(visibilities, transfer, noise_weight, freq_prior):
    vm = pl.BlockSpec(memory_space=pltpu.VMEM)
    hbm = pl.BlockSpec(memory_space=pltpu.HBM)
    dma = pltpu.SemaphoreType.DMA
    out = jax.ShapeDtypeStruct((NF, NM, SIMS, NS), F32)
    slab = pltpu.VMEM((NFQ, OWN, LANES), BF16)
    wide = pltpu.VMEM((NFQ, OWN, LANES), F32)
    right, applied, coef = pl.pallas_call(
        kernel,
        out_shape=(out, out, jax.ShapeDtypeStruct((2, SIMS, 128), F32)),
        in_specs=[hbm] * 5,
        out_specs=(vm, vm, vm),
        scratch_shapes=[
            pltpu.VMEM((NF, NM, NB, NS), BF16),
            pltpu.VMEM((NF, NM, NB, NB), BF16),
            pltpu.VMEM((256, 256), BF16),
            pltpu.VMEM((2, NY, TL, SIMS, HALF), BF16),
            pltpu.VMEM((2, 32, 16, 128), BF16),
            pltpu.VMEM((2, 31, 16, 128), BF16),
            pltpu.VMEM((NF, ROWS, NS), F32),
            pltpu.VMEM((NF, ROWS, NS), F32),
            slab, slab, slab, slab, wide, wide,
            pltpu.VMEM((NFQ, NF, F), F32),
            pltpu.VMEM((2, F * ROWS, F * ROWS), BF16),
            pltpu.VMEM((NF, NB), F32),
            pltpu.VMEM((2, 1, 128), F32),
            pltpu.VMEM((31, 1, 128), F32),
            pltpu.VMEM((7, 1, 128), F32),
            dma((NF,)), dma((5,)), dma((7,)), dma((7,)), dma((2, 3)), dma((2, 3)), dma, dma((2,)),
            dma((7,)), dma((7,)), dma((7,)), dma((7,)), dma((7,)), dma((7,)), dma, dma, dma, dma,
        ],
        compiler_params=pltpu.CompilerParams(
            collective_id=0, has_side_effects=True, vmem_limit_bytes=40 * 1024 * 1024),
    )(*[pltpu.with_memory_space_constraint(v, pltpu.HBM) for v in
        (visibilities, transfer, noise_weight, freq_prior, jnp.asarray(cas_table()))])
    step, ratio = coef[0, :, :1], coef[1, :, :1]
    residual = right - step * applied
    return step * right, residual, residual + ratio * right


def solution(mesh):
    return jax.shard_map(
        local,
        mesh=mesh,
        in_specs=(
            P("ma", "freq", None, None),
            P("freq", "ma", None, None),
            P("freq", None),
            P("freq", None),
        ),
        out_specs=(P("freq", "ma", None, None),) * 3,
        check_vma=False,
    )
```

```python
import math

import jax
import jax.numpy as jnp
import numpy as np
from jax import lax
from jax.experimental import pallas as pl
from jax.experimental.pallas import tpu as pltpu
from jax.sharding import PartitionSpec as P

NZ, NY, NX, NC = 8, 4, 4, 2
NFQ = NX * NC
NF, NM, NB, NS, SIMS, NT, TL = 4, 2, 512, 1024, 4, 512, 16
F = NF * NFQ
ROWS = NM * SIMS
OWN = NF * ROWS
LANES = NS // NFQ
HALF = NB // 2
F32, BF16 = jnp.float32, jnp.bfloat16
HIGH = lax.Precision.HIGHEST
MA_OFFSETS = [(dz, dy) for dz in range(NZ) for dy in range(NY) if dz or dy]
FQ_OFFSETS = [(dx, dc) for dx in range(NX) for dc in range(NC) if dx or dc]


def cas_table():
    m = np.arange(64)
    t = np.arange(NT)
    arg = (m[:, None] * t[None, :]) % NT
    ang = arg.astype(np.float32) * np.float32(2.0 * math.pi / NT)
    cas = (np.cos(ang) + np.sin(ang)) * np.float32(1.0 / math.sqrt(NT))
    cas = cas.reshape(64, NZ, 64).transpose(1, 0, 2)
    eye = np.eye(SIMS, dtype=np.float32)
    full = cas[:, :, None, :, None] * eye[None, None, :, None, :]
    return full.reshape(NZ, 256, 256).astype(jnp.bfloat16)


def dot(a, b, **kw):
    return jnp.dot(a, b, preferred_element_type=F32, **kw)


def dot_t(a, b):
    return lax.dot_general(a, b, (((1,), (1,)), ((), ())), preferred_element_type=F32)


def iota(shape, dim):
    return lax.broadcasted_iota(jnp.int32, shape, dim)


def lane_tiles(v):
    v = sum(v[i * ROWS:(i + 1) * ROWS] for i in range(NF))
    return sum(v[:, i * 128:(i + 1) * 128] for i in range(NS // 128))


def kernel(vis, transfer, weight_hbm, prior_hbm, cas, right_out, applied_out, coef_out,
           tv, gram, casv, vbuf, pbuf, rbuf, right, adj, rsl, rin, asl, ain, csl, cin, prior, spread, weight, dsend, d1, d2,
           tsem, lsem, ps, pr, a1s, a1r, a2s, a2r, rs, rr, as_, ar, cs, cr, d1s, d1r, d2s, d2r, round_sem):
    ma = lax.axis_index("ma")
    fq = lax.axis_index("freq")
    z, y = ma // NY, ma % NY
    x, c = fq // NC, fq % NC

    def ma_peer(dz, dy):
        return lax.rem(z + dz, NZ) * NY + lax.rem(y + dy, NY)

    def fq_peer(dx, dc):
        return lax.rem(x + dx, NX) * NC + lax.rem(c + dc, NC)

    def to_ma(dz, dy):
        return {"ma": ma_peer(dz, dy), "freq": fq}

    def to_fq(dx, dc):
        return {"ma": ma, "freq": fq_peer(dx, dc)}

    tcopies = [pltpu.make_async_copy(transfer.at[f], tv.at[f], tsem.at[f]) for f in range(NF)]
    halves = [pl.ds(h * HALF, HALF) for h in range(2)]
    cas_copy = pltpu.make_async_copy(cas.at[z], casv, lsem.at[0])
    own_vis = [pltpu.make_async_copy(vis.at[:, y, :, halves[h]], vbuf.at[h, y], lsem.at[1 + h]) for h in range(2)]
    own_prior = pltpu.make_async_copy(prior_hbm, prior.at[fq], lsem.at[3])
    own_weight = pltpu.make_async_copy(weight_hbm, weight, lsem.at[4])
    local_copies = [*own_vis, cas_copy, own_prior, own_weight]
    for t in local_copies:
        t.start()

    def greet(sem, ma_offsets, fq_offsets):
        for o in ma_offsets:
            pl.semaphore_signal(sem, 1, device_id=to_ma(*o))
        for o in fq_offsets:
            pl.semaphore_signal(sem, 1, device_id=to_fq(*o))

    near = ([(1, 0), (NZ - 1, 0)], [(1, 0), (NX - 1, 0)])
    barrier = pltpu.get_barrier_semaphore()
    ys = [(0, dy) for dy in range(1, NY)]
    greet(barrier, ys + near[0], near[1] + [(0, 1)])
    pl.semaphore_wait(barrier, len(ys) + 5)
    pending = []

    def send(src, dst, ssem, rsem, peer):
        copy = pltpu.make_async_remote_copy(src, dst, ssem, rsem, device_id=peer)
        copy.start()
        pending.append(copy)
        return copy

    a1 = [[send(vis.at[:, lax.rem(y + dy, NY), :, halves[h]], vbuf.at[h, y], a1s.at[h, dy - 1], a1r.at[h, dy - 1],
                to_ma(0, dy)) for dy in range(1, NY)] for h in range(2)]
    greet(round_sem.at[0], *near)
    for t in tcopies:
        t.start()
    pl.semaphore_wait(round_sem.at[0], 4)
    greet(round_sem.at[1], [(2, 0), (NZ - 2, 0)], [(0, 1)])
    pl.semaphore_wait(round_sem.at[1], 3)
    greet(round_sem.at[2], near[0], [])
    pcs = [send(prior_hbm, prior.at[fq], ps.at[i], pr.at[i], to_fq(*o)) for i, o in enumerate(FQ_OFFSETS)]
    cas_copy.wait()
    pl.semaphore_wait(round_sem.at[2], 2)

    for h in range(2):
        own_vis[h].wait()
        for r in a1[h]:
            r.wait_recv()
        part = dot(casv[...], vbuf[h].reshape(256, HALF)).reshape(32, ROWS, HALF)
        pbuf[h] = jnp.concatenate([part[:, :, :128], part[:, :, 128:]], axis=1).astype(BF16)
        for dz, dy in MA_OFFSETS:
            send(pbuf.at[h, ma_peer(dz, dy)], rbuf.at[h, dz * NY + dy - 1], a2s, a2r.at[h], to_ma(dz, dy))

    own_prior.wait()
    own_weight.wait()
    for r in pcs:
        r.wait_recv()
    e1 = (iota((F * ROWS, F), 0) // ROWS == iota((F * ROWS, F), 1)).astype(F32)
    e2 = (iota((F, F * ROWS), 0) == iota((F, F * ROWS), 1) // ROWS).astype(F32)
    full = dot(dot(e1, prior[...].reshape(F, F), precision=HIGH), e2, precision=HIGH)
    same = iota((F * ROWS, F * ROWS), 0) % ROWS == iota((F * ROWS, F * ROWS), 1) % ROWS
    full = jnp.where(same, full, 0.0)
    spread[0] = full.astype(BF16)
    spread[1] = (full - full.astype(BF16).astype(F32)).astype(BF16)
    for t in tcopies:
        t.wait()

    @pl.loop(0, NF)
    def _(f):
        for m in range(NM):
            block = tv[f, m]
            gram[f, m] = dot_t(block, block).astype(BF16)

    low = iota((ROWS, 1), 0) < SIMS

    def both(a, ref, f, at=slice(None)):
        return jnp.where(low, dot(a, ref[f, 0, at]), dot(a, ref[f, 1, at]))

    acc, obs = [None] * NY, [None] * NY
    for h in range(2):
        pltpu.make_async_copy(rbuf.at[h], rbuf.at[h], a2r.at[h]).wait()
        for dy in range(NY):
            f = lax.rem(y + NY - dy, NY)
            total = None
            for dz in range(NZ):
                slot = dz * NY + dy
                piece = pbuf[h, ma] if slot == 0 else rbuf[h, slot - 1]
                piece = piece.astype(F32)
                total = piece if total is None else total + piece
            modes = jnp.concatenate([total[:ROWS], total[ROWS:]], axis=1)
            weighted = (weight[pl.ds(f, 1), halves[h]] * modes).astype(BF16)
            out = both(weighted, tv, f, halves[h])
            acc[dy] = out if h == 0 else acc[dy] + out
            out = both(weighted, gram, f, halves[h])
            obs[dy] = out if h == 0 else obs[dy] + out
    for dy in range(NY):
        right[lax.rem(y + NY - dy, NY)] = acc[dy]

    def slices(v, ref):
        v = v.astype(BF16)
        for j in range(NFQ):
            ref[j] = v[:, j * LANES:(j + 1) * LANES]

    rt = right[...].reshape(OWN, NS)
    slices(rt, rsl)
    rc = [send(rsl.at[fq_peer(*o)], rin.at[fq], rs.at[i], rr.at[i], to_fq(*o)) for i, o in enumerate(FQ_OFFSETS)]
    rin[fq] = rsl[fq]

    for dy in range(NY):
        f = lax.rem(y + NY - dy, NY)
        scaled = (weight[pl.ds(f, 1), :] * obs[dy]).astype(BF16)
        adj[f] = both(scaled, tv, f)
    at = adj[...].reshape(OWN, NS)
    slices(at, asl)
    ac = [send(asl.at[fq_peer(*o)], ain.at[fq], as_.at[i], ar.at[i], to_fq(*o)) for i, o in enumerate(FQ_OFFSETS)]
    ain[fq] = asl[fq]

    for r in rc:
        r.wait_recv()
    rall = rin[...].reshape(F * ROWS, LANES)
    coupled = dot(spread[...].reshape(2 * F * ROWS, F * ROWS), rall)
    coupled = coupled[:F * ROWS] + coupled[F * ROWS:]
    csl[...] = coupled.reshape(NFQ, OWN, LANES)
    cc = [send(csl.at[fq_peer(*o)], cin.at[fq], cs.at[i], cr.at[i], to_fq(*o)) for i, o in enumerate(FQ_OFFSETS)]
    cin[fq] = csl[fq]

    def blocks(v):
        return sum(v[i * ROWS:(i + 1) * ROWS] for i in range(F))

    n = lane_tiles(rt * rt)
    cu = lane_tiles(rt * at) + blocks(rall.astype(F32) * coupled)
    q = lane_tiles(at * at)
    for r in ac:
        r.wait_recv()
    q = q + blocks((2.0 * ain[...].reshape(F * ROWS, LANES).astype(F32) + coupled) * coupled)

    row, lane = iota((ROWS, 128), 0), iota((ROWS, 128), 1)

    def put(v, at_lane):
        return jnp.where(lane == row + at_lane, jnp.sum(v, axis=1, keepdims=True), 0.0)

    own = jnp.sum(put(n, 0) + put(cu, ROWS) + put(q, 2 * ROWS), axis=0, keepdims=True)
    dsend[0] = own
    for i, o in enumerate(MA_OFFSETS):
        send(dsend.at[0], d1.at[i], d1s, d1r, to_ma(*o))
    for f in range(NF):
        for m in range(NM):
            right_out[f, m] = right[f, m * SIMS:(m + 1) * SIMS]
    pltpu.make_async_copy(d1, d1, d1r).wait()
    own = own + jnp.sum(d1[...], axis=0)
    dsend[1] = own
    for i, o in enumerate(FQ_OFFSETS):
        send(dsend.at[1], d2.at[i], d2s, d2r, to_fq(*o))
    for r in cc:
        r.wait_recv()
    for f in range(NF):
        coup = jnp.concatenate([cin[j, f * ROWS:(f + 1) * ROWS] for j in range(NFQ)], axis=1)
        applied = adj[f] + coup
        for m in range(NM):
            applied_out[f, m] = applied[m * SIMS:(m + 1) * SIMS]
    pltpu.make_async_copy(d2, d2, d2r).wait()
    own = own + jnp.sum(d2[...], axis=0)

    def take(at_lane):
        inside = (lane >= at_lane) & (lane < at_lane + ROWS) & (lane % SIMS == row % SIMS)
        return jnp.sum(jnp.where(inside, own, 0.0), axis=1, keepdims=True)

    norm, curve, image = take(0), take(ROWS), take(2 * ROWS)
    step = norm / curve
    ratio = (image / curve) * step - 1.0
    coef_out[0] = jnp.broadcast_to(step[:SIMS], (SIMS, 128))
    coef_out[1] = jnp.broadcast_to(ratio[:SIMS], (SIMS, 128))
    for r in pending:
        r.wait_send()


def local(visibilities, transfer, noise_weight, freq_prior):
    vm = pl.BlockSpec(memory_space=pltpu.VMEM)
    hbm = pl.BlockSpec(memory_space=pltpu.HBM)
    dma = pltpu.SemaphoreType.DMA
    out = jax.ShapeDtypeStruct((NF, NM, SIMS, NS), F32)
    slab = pltpu.VMEM((NFQ, OWN, LANES), BF16)
    wide = pltpu.VMEM((NFQ, OWN, LANES), F32)
    right, applied, coef = pl.pallas_call(
        kernel,
        out_shape=(out, out, jax.ShapeDtypeStruct((2, SIMS, 128), F32)),
        in_specs=[hbm] * 5,
        out_specs=(vm, vm, vm),
        scratch_shapes=[
            pltpu.VMEM((NF, NM, NB, NS), BF16),
            pltpu.VMEM((NF, NM, NB, NB), BF16),
            pltpu.VMEM((256, 256), BF16),
            pltpu.VMEM((2, NY, TL, SIMS, HALF), BF16),
            pltpu.VMEM((2, 32, 16, 128), BF16),
            pltpu.VMEM((2, 31, 16, 128), BF16),
            pltpu.VMEM((NF, ROWS, NS), F32),
            pltpu.VMEM((NF, ROWS, NS), F32),
            slab, slab, slab, slab, wide, wide,
            pltpu.VMEM((NFQ, NF, F), F32),
            pltpu.VMEM((2, F * ROWS, F * ROWS), BF16),
            pltpu.VMEM((NF, NB), F32),
            pltpu.VMEM((2, 1, 128), F32),
            pltpu.VMEM((31, 1, 128), F32),
            pltpu.VMEM((7, 1, 128), F32),
            dma((NF,)), dma((5,)), dma((7,)), dma((7,)), dma((2, 3)), dma((2, 3)), dma, dma((2,)),
            dma((7,)), dma((7,)), dma((7,)), dma((7,)), dma((7,)), dma((7,)), dma, dma, dma, dma,
            pltpu.SemaphoreType.REGULAR((3,)),
        ],
        compiler_params=pltpu.CompilerParams(
            collective_id=0, has_side_effects=True, vmem_limit_bytes=40 * 1024 * 1024),
    )(*[pltpu.with_memory_space_constraint(v, pltpu.HBM) for v in
        (visibilities, transfer, noise_weight, freq_prior, jnp.asarray(cas_table()))])
    step, ratio = coef[0, :, :1], coef[1, :, :1]
    residual = right - step * applied
    return step * right, residual, residual + ratio * right


def solution(mesh):
    return jax.shard_map(
        local,
        mesh=mesh,
        in_specs=(
            P("ma", "freq", None, None),
            P("freq", "ma", None, None),
            P("freq", None),
            P("freq", None),
        ),
        out_specs=(P("freq", "ma", None, None),) * 3,
        check_vma=False,
    )
```

```python
import math

import jax
import jax.numpy as jnp
import numpy as np
from jax import lax
from jax.experimental import pallas as pl
from jax.experimental.pallas import tpu as pltpu
from jax.sharding import PartitionSpec as P

NZ, NY, NX, NC = 8, 4, 4, 2
NFQ = NX * NC
NF, NM, NB, NS, SIMS, NT, TL = 4, 2, 512, 1024, 4, 512, 16
F = NF * NFQ
ROWS = NM * SIMS
OWN = NF * ROWS
LANES = NS // NFQ
HALF = NB // 2
F32, BF16 = jnp.float32, jnp.bfloat16
HIGH = lax.Precision.HIGHEST
MA_GROUPS = [[(dz, dy) for dz in zs for dy in (2, 1, 3, 0) if dz or dy] for zs in ((3, 5, 1, 7), (4, 2, 6, 0))]
MA_OFFSETS = MA_GROUPS[1] + MA_GROUPS[0]
FQ_OFFSETS = [(dx, dc) for dx in range(NX) for dc in range(NC) if dx or dc]


def cas_table():
    m = np.arange(64)
    t = np.arange(NT)
    arg = (m[:, None] * t[None, :]) % NT
    ang = arg.astype(np.float32) * np.float32(2.0 * math.pi / NT)
    cas = (np.cos(ang) + np.sin(ang)) * np.float32(1.0 / math.sqrt(NT))
    cas = cas.reshape(64, NZ // 2, 128).transpose(1, 0, 2)
    eye = np.eye(SIMS, dtype=np.float32)
    full = cas[:, :, None, :, None] * eye[None, None, :, None, :]
    return full.reshape(NZ // 2, 256, 512).astype(jnp.bfloat16)


def dot(a, b, **kw):
    return jnp.dot(a, b, preferred_element_type=F32, **kw)


def dot_t(a, b):
    return lax.dot_general(a, b, (((1,), (1,)), ((), ())), preferred_element_type=F32)


def iota(shape, dim):
    return lax.broadcasted_iota(jnp.int32, shape, dim)


def lane_tiles(v):
    v = sum(v[i * ROWS:(i + 1) * ROWS] for i in range(NF))
    return sum(v[:, i * 128:(i + 1) * 128] for i in range(NS // 128))


def kernel(vis, transfer, weight_hbm, prior_hbm, cas, right_out, applied_out, step_out, ratio_out,
           tv, turned, casv, vbuf, pbuf, rbuf0, rbuf1, right, adj, rsl, rin, asl, ain, csl, cin, prior, spread, weight, dsend, d1, d2,
           tsem, lsem, ps, pr, a1s, a1r, a2s, a2r, rs, rr, as_, ar, cs, cr, d1s, d1r, d2s, d2r, round_sem):
    ma = lax.axis_index("ma")
    fq = lax.axis_index("freq")
    z, y = ma // NY, ma % NY
    rbuf = (rbuf0, rbuf1)
    x, c = fq // NC, fq % NC

    def ma_peer(dz, dy):
        return lax.rem(z + dz, NZ) * NY + lax.rem(y + dy, NY)

    def fq_peer(dx, dc):
        return lax.rem(x + dx, NX) * NC + lax.rem(c + dc, NC)

    def to_ma(dz, dy):
        return {"ma": ma_peer(dz, dy), "freq": fq}

    def to_fq(dx, dc):
        return {"ma": ma, "freq": fq_peer(dx, dc)}

    tcopies = [pltpu.make_async_copy(transfer.at[f], tv.at[f], tsem.at[f]) for f in range(NF)]
    odd = z % 2
    mate = z + 1 - 2 * odd
    other = lax.rem(z + NZ - 1 + 2 * odd, NZ)

    def half(h):
        return pl.ds(pl.multiple_of(h * HALF, HALF), HALF)

    cas_copy = pltpu.make_async_copy(cas.at[z // 2], casv, lsem.at[0])
    own_vis = [pltpu.make_async_copy(vis.at[:, y, :, half(odd)], vbuf.at[odd, y], lsem.at[1])]
    own_prior = pltpu.make_async_copy(prior_hbm, prior.at[fq], lsem.at[3])
    own_weight = pltpu.make_async_copy(weight_hbm, weight, lsem.at[4])
    local_copies = [*own_vis, cas_copy, own_prior, own_weight]
    for t in local_copies:
        t.start()

    def greet(sem, ma_offsets, fq_offsets):
        for o in ma_offsets:
            pl.semaphore_signal(sem, 1, device_id=to_ma(*o))
        for o in fq_offsets:
            pl.semaphore_signal(sem, 1, device_id=to_fq(*o))

    def at_z(zz, dy):
        return {"ma": zz * NY + lax.rem(y + dy, NY), "freq": fq}

    near = ([(1, 0), (NZ - 1, 0)], [(1, 0), (NX - 1, 0)])
    pair = [at_z(mate, dy) for dy in range(NY)] + [at_z(z, dy) for dy in range(1, NY)]
    barrier = pltpu.get_barrier_semaphore()
    for peer in pair + [at_z(other, 0)]:
        pl.semaphore_signal(barrier, 1, device_id=peer)
    greet(barrier, [], near[1] + [(0, 1)])
    pl.semaphore_wait(barrier, len(pair) + 4)
    pending = []

    def send(src, dst, ssem, rsem, peer):
        copy = pltpu.make_async_remote_copy(src, dst, ssem, rsem, device_id=peer)
        copy.start()
        pending.append(copy)
        return copy

    a1 = []
    for i, (peer, h, dy) in enumerate([(at_z(mate, dy), 1 - odd, dy) for dy in range(NY)] + [(at_z(z, dy), odd, dy) for dy in range(1, NY)]):
        a1.append(send(vis.at[:, lax.rem(y + dy, NY), :, half(h)], vbuf.at[odd, y], a1s.at[i], a1r.at[i], peer))
    greet(round_sem.at[0], *near)
    for t in tcopies:
        t.start()
    pl.semaphore_wait(round_sem.at[0], 4)
    greet(round_sem.at[1], [(2, 0), (NZ - 2, 0)], [(0, 1)])
    pl.semaphore_wait(round_sem.at[1], 3)
    greet(round_sem.at[2], near[0], [])
    pcs = [send(prior_hbm, prior.at[fq], ps.at[i], pr.at[i], to_fq(*o)) for i, o in enumerate(FQ_OFFSETS)]
    cas_copy.wait()
    pl.semaphore_wait(round_sem.at[2], 2)

    own_vis[0].wait()
    for r in a1:
        r.wait_recv()
    part = dot(casv[...], vbuf[...].reshape(512, HALF)).reshape(32, ROWS, HALF)
    pbuf[...] = jnp.concatenate([part[:, :, :128], part[:, :, 128:]], axis=1).astype(BF16)
    for h in range(2):
        for i, o in enumerate(MA_GROUPS[h]):
            send(pbuf.at[ma_peer(*o)], rbuf[h].at[i], a2s, a2r.at[h], to_ma(*o))

    own_prior.wait()
    own_weight.wait()
    for r in pcs:
        r.wait_recv()
    e1 = (iota((F * ROWS, F), 0) // ROWS == iota((F * ROWS, F), 1)).astype(F32)
    e2 = (iota((F, F * ROWS), 0) == iota((F, F * ROWS), 1) // ROWS).astype(F32)
    full = dot(dot(e1, prior[...].reshape(F, F), precision=HIGH), e2, precision=HIGH)
    same = iota((F * ROWS, F * ROWS), 0) % ROWS == iota((F * ROWS, F * ROWS), 1) % ROWS
    full = jnp.where(same, full, 0.0)
    spread[0] = full.astype(BF16)
    spread[1] = (full - full.astype(BF16).astype(F32)).astype(BF16)
    for t in tcopies:
        t.wait()

    @pl.loop(0, NF)
    def _(f):
        for m in range(NM):
            turned[f, m] = tv[f, m].T

    low = iota((ROWS, 1), 0) < SIMS

    def both(a, ref, f, at=slice(None)):
        return jnp.where(low, dot(a, ref[f, 0, at]), dot(a, ref[f, 1, at]))

    acc = [None] * NY
    for h in range(2):
        pltpu.make_async_copy(rbuf[h], rbuf[h], a2r.at[h]).wait()
        rows = half(1 - odd if h == 0 else odd)
        for dy in range(NY):
            f = lax.rem(y + NY - dy, NY)
            pieces = [rbuf[h][i] for i, o in enumerate(MA_GROUPS[h]) if o[1] == dy]
            if h == 1 and dy == 0:
                pieces.append(pbuf[ma])
            total = sum(p.astype(F32) for p in pieces)
            modes = jnp.concatenate([total[:ROWS], total[ROWS:]], axis=1)
            weighted = (weight[pl.ds(f, 1), rows] * modes).astype(BF16)
            out = both(weighted, tv, f, rows)
            acc[dy] = out if h == 0 else acc[dy] + out
    for dy in range(NY):
        right[lax.rem(y + NY - dy, NY)] = acc[dy]

    def slices(v, ref):
        v = v.astype(BF16)
        for j in range(NFQ):
            ref[j] = v[:, j * LANES:(j + 1) * LANES]

    rt = right[...].reshape(OWN, NS)
    slices(rt, rsl)
    rc = [send(rsl.at[fq_peer(*o)], rin.at[fq], rs.at[i], rr.at[i], to_fq(*o)) for i, o in enumerate(FQ_OFFSETS)]
    rin[fq] = rsl[fq]

    for dy in range(NY):
        f = lax.rem(y + NY - dy, NY)
        observed = both(acc[dy].astype(BF16), turned, f)
        scaled = (weight[pl.ds(f, 1), :] * observed).astype(BF16)
        adj[f] = both(scaled, tv, f)
    at = adj[...].reshape(OWN, NS)
    slices(at, asl)
    ac = [send(asl.at[fq_peer(*o)], ain.at[fq], as_.at[i], ar.at[i], to_fq(*o)) for i, o in enumerate(FQ_OFFSETS)]
    ain[fq] = asl[fq]

    for r in rc:
        r.wait_recv()
    rall = rin[...].reshape(F * ROWS, LANES)
    coupled = dot(spread[...].reshape(2 * F * ROWS, F * ROWS), rall)
    coupled = coupled[:F * ROWS] + coupled[F * ROWS:]
    csl[...] = coupled.reshape(NFQ, OWN, LANES)
    cc = [send(csl.at[fq_peer(*o)], cin.at[fq], cs.at[i], cr.at[i], to_fq(*o)) for i, o in enumerate(FQ_OFFSETS)]
    cin[fq] = csl[fq]

    def blocks(v):
        return sum(v[i * ROWS:(i + 1) * ROWS] for i in range(F))

    row, lane = iota((ROWS, 128), 0), iota((ROWS, 128), 1)

    def put(v, at_lane):
        return jnp.where(lane == row + at_lane, jnp.sum(v, axis=1, keepdims=True), 0.0)

    rest = put(lane_tiles(rt * rt), 0) + put(lane_tiles(rt * at) + blocks(rall.astype(F32) * coupled), ROWS)
    image = lane_tiles(at * at) + blocks(coupled * coupled)
    for r in ac:
        r.wait_recv()
    image = image + blocks(2.0 * ain[...].reshape(F * ROWS, LANES).astype(F32) * coupled)

    own = jnp.sum(rest + put(image, 2 * ROWS), axis=0, keepdims=True)
    dsend[0] = own
    for i, o in enumerate(MA_OFFSETS):
        send(dsend.at[0], d1.at[i], d1s, d1r, to_ma(*o))
    for f in range(NF):
        for m in range(NM):
            right_out[f, m] = right[f, m * SIMS:(m + 1) * SIMS]
    pltpu.make_async_copy(d1, d1, d1r).wait()
    own = own + jnp.sum(d1[...], axis=0)
    dsend[1] = own
    for i, o in enumerate(FQ_OFFSETS):
        send(dsend.at[1], d2.at[i], d2s, d2r, to_fq(*o))
    for r in cc:
        r.wait_recv()
    for f in range(NF):
        coup = jnp.concatenate([cin[j, f * ROWS:(f + 1) * ROWS] for j in range(NFQ)], axis=1)
        applied = adj[f] + coup
        for m in range(NM):
            applied_out[f, m] = applied[m * SIMS:(m + 1) * SIMS]
    pltpu.make_async_copy(d2, d2, d2r).wait()
    own = own + jnp.sum(d2[...], axis=0)

    def take(at_lane):
        inside = (lane >= at_lane) & (lane < at_lane + ROWS) & (lane % SIMS == row % SIMS)
        return jnp.sum(jnp.where(inside, own, 0.0), axis=1, keepdims=True)

    norm, curve, image = take(0), take(ROWS), take(2 * ROWS)
    step = norm / curve
    ratio = (image / curve) * step - 1.0
    step_out[...] = jnp.broadcast_to(step[:SIMS], (SIMS, NS))
    ratio_out[...] = jnp.broadcast_to(ratio[:SIMS], (SIMS, NS))
    for r in pending:
        r.wait_send()


def local(visibilities, transfer, noise_weight, freq_prior):
    vm = pl.BlockSpec(memory_space=pltpu.VMEM)
    hbm = pl.BlockSpec(memory_space=pltpu.HBM)
    dma = pltpu.SemaphoreType.DMA
    out = jax.ShapeDtypeStruct((NF, NM, SIMS, NS), F32)
    coef = jax.ShapeDtypeStruct((SIMS, NS), F32)
    slab = pltpu.VMEM((NFQ, OWN, LANES), BF16)
    wide = pltpu.VMEM((NFQ, OWN, LANES), F32)
    right, applied, step, ratio = pl.pallas_call(
        kernel,
        out_shape=(out, out, coef, coef),
        in_specs=[hbm] * 5,
        out_specs=(vm,) * 4,
        scratch_shapes=[
            pltpu.VMEM((NF, NM, NB, NS), BF16),
            pltpu.VMEM((NF, NM, NS, NB), BF16),
            pltpu.VMEM((256, 512), BF16),
            pltpu.VMEM((2, NY, TL, SIMS, HALF), BF16),
            pltpu.VMEM((32, 16, 128), BF16),
            pltpu.VMEM((16, 16, 128), BF16),
            pltpu.VMEM((15, 16, 128), BF16),
            pltpu.VMEM((NF, ROWS, NS), F32),
            pltpu.VMEM((NF, ROWS, NS), F32),
            slab, slab, slab, slab, wide, wide,
            pltpu.VMEM((NFQ, NF, F), F32),
            pltpu.VMEM((2, F * ROWS, F * ROWS), BF16),
            pltpu.VMEM((NF, NB), F32),
            pltpu.VMEM((2, 1, 128), F32),
            pltpu.VMEM((31, 1, 128), F32),
            pltpu.VMEM((7, 1, 128), F32),
            dma((NF,)), dma((5,)), dma((7,)), dma((7,)), dma((7,)), dma((7,)), dma, dma((2,)),
            dma((7,)), dma((7,)), dma((7,)), dma((7,)), dma((7,)), dma((7,)), dma, dma, dma, dma,
            pltpu.SemaphoreType.REGULAR((3,)),
        ],
        compiler_params=pltpu.CompilerParams(
            collective_id=0, has_side_effects=True, vmem_limit_bytes=40 * 1024 * 1024),
    )(*[pltpu.with_memory_space_constraint(v, pltpu.HBM) for v in
        (visibilities, transfer, noise_weight, freq_prior, jnp.asarray(cas_table()))])
    residual = right - step * applied
    return step * right, residual, residual + ratio * right


def solution(mesh):
    return jax.shard_map(
        local,
        mesh=mesh,
        in_specs=(
            P("ma", "freq", None, None),
            P("freq", "ma", None, None),
            P("freq", None),
            P("freq", None),
        ),
        out_specs=(P("freq", "ma", None, None),) * 3,
        check_vma=False,
    )
```

```python
import math

import jax
import jax.numpy as jnp
import numpy as np
from jax import lax
from jax.experimental import pallas as pl
from jax.experimental.pallas import tpu as pltpu
from jax.sharding import PartitionSpec as P

NZ, NY, NX, NC = 8, 4, 4, 2
NFQ = NX * NC
NF, NM, NB, NS, SIMS, NT, TL = 4, 2, 512, 1024, 4, 512, 16
F = NF * NFQ
ROWS = NM * SIMS
OWN = NF * ROWS
LANES = NS // NFQ
HALF = NB // 2
F32, BF16 = jnp.float32, jnp.bfloat16
HIGH = lax.Precision.HIGHEST
MA_GROUPS = [[(dz, dy) for dz in zs for dy in (2, 1, 3, 0) if dz or dy] for zs in ((3, 5, 1, 7), (4, 2, 6, 0))]
MA_OFFSETS = sorted(MA_GROUPS[0] + MA_GROUPS[1], key=lambda o: -min(o[0], NZ - o[0]) - min(o[1], NY - o[1]))
FQ_OFFSETS = [(dx, dc) for dx in range(NX) for dc in range(NC) if dx or dc]


def cas_table():
    m = np.arange(64)
    t = np.arange(NT)
    arg = (m[:, None] * t[None, :]) % NT
    ang = arg.astype(np.float32) * np.float32(2.0 * math.pi / NT)
    cas = (np.cos(ang) + np.sin(ang)) * np.float32(1.0 / math.sqrt(NT))
    cas = cas.reshape(64, NZ // 2, 128).transpose(1, 0, 2)
    eye = np.eye(SIMS, dtype=np.float32)
    full = cas[:, :, None, :, None] * eye[None, None, :, None, :]
    return full.reshape(NZ // 2, 256, 512).astype(jnp.bfloat16)


def dot(a, b, **kw):
    return jnp.dot(a, b, preferred_element_type=F32, **kw)


def dot_t(a, b):
    return lax.dot_general(a, b, (((1,), (1,)), ((), ())), preferred_element_type=F32)


def iota(shape, dim):
    return lax.broadcasted_iota(jnp.int32, shape, dim)


def lane_tiles(v):
    v = sum(v[i * ROWS:(i + 1) * ROWS] for i in range(NF))
    return sum(v[:, i * 128:(i + 1) * 128] for i in range(NS // 128))


def kernel(vis, transfer, weight_hbm, prior_hbm, cas, right_out, applied_out, step_out, ratio_out,
           tv, turned, casv, vbuf, pbuf, rbuf0, rbuf1, right, adj, rsl, rin, asl, ain, csl, cin, prior, spread, weight, dsend, d1, d2,
           tsem, lsem, ps, pr, a1s, a1r, a2s, a2r, rs, rr, as_, ar, cs, cr, d1s, d1r, d2s, d2r, round_sem):
    ma = lax.axis_index("ma")
    fq = lax.axis_index("freq")
    z, y = ma // NY, ma % NY
    rbuf = (rbuf0, rbuf1)
    x, c = fq // NC, fq % NC

    def ma_peer(dz, dy):
        return lax.rem(z + dz, NZ) * NY + lax.rem(y + dy, NY)

    def fq_peer(dx, dc):
        return lax.rem(x + dx, NX) * NC + lax.rem(c + dc, NC)

    def to_ma(dz, dy):
        return {"ma": ma_peer(dz, dy), "freq": fq}

    def to_fq(dx, dc):
        return {"ma": ma, "freq": fq_peer(dx, dc)}

    tcopies = [pltpu.make_async_copy(transfer.at[f], tv.at[f], tsem.at[f]) for f in range(NF)]
    odd = z % 2
    mate = z + 1 - 2 * odd
    other = lax.rem(z + NZ - 1 + 2 * odd, NZ)

    def half(h):
        return pl.ds(pl.multiple_of(h * HALF, HALF), HALF)

    cas_copy = pltpu.make_async_copy(cas.at[z // 2], casv, lsem.at[0])
    own_vis = [pltpu.make_async_copy(vis.at[:, y, :, half(odd)], vbuf.at[odd, y], lsem.at[1])]
    own_prior = pltpu.make_async_copy(prior_hbm, prior.at[fq], lsem.at[3])
    own_weight = pltpu.make_async_copy(weight_hbm, weight, lsem.at[4])
    local_copies = [*own_vis, cas_copy, own_prior, own_weight]

    def greet(sem, ma_offsets, fq_offsets):
        for o in ma_offsets:
            pl.semaphore_signal(sem, 1, device_id=to_ma(*o))
        for o in fq_offsets:
            pl.semaphore_signal(sem, 1, device_id=to_fq(*o))

    def at_z(zz, dy):
        return {"ma": zz * NY + lax.rem(y + dy, NY), "freq": fq}

    near = ([(1, 0), (NZ - 1, 0)], [(1, 0), (NX - 1, 0)])
    pair = [at_z(mate, dy) for dy in range(NY)] + [at_z(z, dy) for dy in range(1, NY)]
    barrier = pltpu.get_barrier_semaphore()
    for peer in pair + [at_z(other, 0)]:
        pl.semaphore_signal(barrier, 1, device_id=peer)
    greet(barrier, [], near[1] + [(0, 1)])
    for t in local_copies + tcopies:
        t.start()
    pl.semaphore_wait(barrier, len(pair) + 4)
    pending = []

    def send(src, dst, ssem, rsem, peer):
        copy = pltpu.make_async_remote_copy(src, dst, ssem, rsem, device_id=peer)
        copy.start()
        pending.append(copy)
        return copy

    def drain():
        for copy in pending:
            copy.wait_send()
        pending.clear()

    a1 = []
    for i, (peer, h, dy) in enumerate([(at_z(mate, 2), 1 - odd, 2), (at_z(z, 2), odd, 2), (at_z(mate, 1), 1 - odd, 1), (at_z(mate, 3), 1 - odd, 3),
                                              (at_z(z, 1), odd, 1), (at_z(z, 3), odd, 3), (at_z(mate, 0), 1 - odd, 0)]):
        a1.append(send(vis.at[:, lax.rem(y + dy, NY), :, half(h)], vbuf.at[odd, y], a1s.at[i], a1r.at[i], peer))
    greet(round_sem.at[0], *near)
    pl.semaphore_wait(round_sem.at[0], 4)
    greet(round_sem.at[1], [(2, 0), (NZ - 2, 0)], [(0, 1)])
    pl.semaphore_wait(round_sem.at[1], 3)
    greet(round_sem.at[2], near[0], [])
    pcs = [send(prior_hbm, prior.at[fq], ps.at[i], pr.at[i], to_fq(*o)) for i, o in enumerate(FQ_OFFSETS)]
    cas_copy.wait()
    pl.semaphore_wait(round_sem.at[2], 2)

    own_vis[0].wait()
    for r in a1:
        r.wait_recv()
    part = dot(casv[...], vbuf[...].reshape(512, HALF)).reshape(32, ROWS, HALF)
    pbuf[...] = jnp.concatenate([part[:, :, :128], part[:, :, 128:]], axis=1).astype(BF16)
    for h in range(2):
        for i, o in enumerate(MA_GROUPS[h]):
            pltpu.make_async_remote_copy(pbuf.at[ma_peer(*o)], rbuf[h].at[i], a2s.at[h], a2r.at[h], device_id=to_ma(*o)).start()

    own_prior.wait()
    own_weight.wait()
    for r in pcs:
        r.wait_recv()
    e1 = (iota((F * ROWS, F), 0) // ROWS == iota((F * ROWS, F), 1)).astype(F32)
    e2 = (iota((F, F * ROWS), 0) == iota((F, F * ROWS), 1) // ROWS).astype(F32)
    full = dot(dot(e1, prior[...].reshape(F, F), precision=HIGH), e2, precision=HIGH)
    same = iota((F * ROWS, F * ROWS), 0) % ROWS == iota((F * ROWS, F * ROWS), 1) % ROWS
    full = jnp.where(same, full, 0.0)
    spread[0] = full.astype(BF16)
    spread[1] = (full - full.astype(BF16).astype(F32)).astype(BF16)
    for t in tcopies:
        t.wait()

    @pl.loop(0, NF)
    def _(f):
        for m in range(NM):
            turned[f, m] = tv[f, m].T

    low = iota((ROWS, 1), 0) < SIMS

    def both(a, ref, f, at=slice(None)):
        return jnp.where(low, dot(a, ref[f, 0, at]), dot(a, ref[f, 1, at]))

    acc = [None] * NY
    for h in range(2):
        pltpu.make_async_copy(rbuf[h], rbuf[h], a2r.at[h]).wait()
        rows = half(1 - odd if h == 0 else odd)
        for dy in range(NY):
            f = lax.rem(y + NY - dy, NY)
            pieces = [rbuf[h][i] for i, o in enumerate(MA_GROUPS[h]) if o[1] == dy]
            if h == 1 and dy == 0:
                pieces.append(pbuf[ma])
            total = sum(p.astype(F32) for p in pieces)
            modes = jnp.concatenate([total[:ROWS], total[ROWS:]], axis=1)
            weighted = (weight[pl.ds(f, 1), rows] * modes).astype(BF16)
            out = both(weighted, tv, f, rows)
            acc[dy] = out if h == 0 else acc[dy] + out
    for dy in range(NY):
        right[lax.rem(y + NY - dy, NY)] = acc[dy]

    def slices(v, ref):
        v = v.astype(BF16)
        for j in range(NFQ):
            ref[j] = v[:, j * LANES:(j + 1) * LANES]

    rt = right[...].reshape(OWN, NS)
    slices(rt, rsl)
    rc = [send(rsl.at[fq_peer(*o)], rin.at[fq], rs.at[i], rr.at[i], to_fq(*o)) for i, o in enumerate(FQ_OFFSETS)]
    rin[fq] = rsl[fq]

    for dy in range(NY):
        f = lax.rem(y + NY - dy, NY)
        observed = both(acc[dy].astype(BF16), turned, f)
        scaled = (weight[pl.ds(f, 1), :] * observed).astype(BF16)
        adj[f] = both(scaled, tv, f)
    at = adj[...].reshape(OWN, NS)
    slices(at, asl)
    ac = [send(asl.at[fq_peer(*o)], ain.at[fq], as_.at[i], ar.at[i], to_fq(*o)) for i, o in enumerate(FQ_OFFSETS)]
    ain[fq] = asl[fq]

    for r in rc:
        r.wait_recv()
    rall = rin[...].reshape(F * ROWS, LANES)
    coupled = dot(spread[...].reshape(2 * F * ROWS, F * ROWS), rall)
    coupled = coupled[:F * ROWS] + coupled[F * ROWS:]

    def blocks(v):
        return sum(v[i * ROWS:(i + 1) * ROWS] for i in range(F))

    row, lane = iota((ROWS, 128), 0), iota((ROWS, 128), 1)

    def put(v, at_lane):
        return jnp.where(lane == row + at_lane, jnp.sum(v, axis=1, keepdims=True), 0.0)

    rest = put(lane_tiles(rt * rt), 0) + put(lane_tiles(rt * at) + blocks(rall.astype(F32) * coupled), ROWS)
    image = lane_tiles(at * at) + blocks(coupled * coupled)
    for r in ac:
        r.wait_recv()
    image = image + blocks(2.0 * ain[...].reshape(F * ROWS, LANES).astype(F32) * coupled)

    own = jnp.sum(rest + put(image, 2 * ROWS), axis=0, keepdims=True)
    dsend[0] = own
    for i, o in enumerate(MA_OFFSETS):
        pltpu.make_async_remote_copy(dsend.at[0], d1.at[i], d1s, d1r, device_id=to_ma(*o)).start()
    csl[...] = coupled.reshape(NFQ, OWN, LANES)
    cc = [send(csl.at[fq_peer(*o)], cin.at[fq], cs.at[i], cr.at[i], to_fq(*o)) for i, o in enumerate(FQ_OFFSETS)]
    cin[fq] = csl[fq]
    for f in range(NF):
        for m in range(NM):
            right_out[f, m] = right[f, m * SIMS:(m + 1) * SIMS]
    drain()
    for h in range(2):
        pltpu.make_async_copy(rbuf[h], rbuf[h], a2s.at[h]).wait()
    pltpu.make_async_copy(d1, d1, d1s).wait()
    pltpu.make_async_copy(d1, d1, d1r).wait()
    own = own + jnp.sum(d1[...], axis=0)
    dsend[1] = own
    for i, o in enumerate(FQ_OFFSETS):
        send(dsend.at[1], d2.at[i], d2s, d2r, to_fq(*o))
    for r in cc:
        r.wait_recv()
    for f in range(NF):
        coup = jnp.concatenate([cin[j, f * ROWS:(f + 1) * ROWS] for j in range(NFQ)], axis=1)
        applied = adj[f] + coup
        for m in range(NM):
            applied_out[f, m] = applied[m * SIMS:(m + 1) * SIMS]
    pltpu.make_async_copy(d2, d2, d2r).wait()
    own = own + jnp.sum(d2[...], axis=0)

    def take(at_lane):
        inside = (lane >= at_lane) & (lane < at_lane + ROWS) & (lane % SIMS == row % SIMS)
        return jnp.sum(jnp.where(inside, own, 0.0), axis=1, keepdims=True)

    norm, curve, image = take(0), take(ROWS), take(2 * ROWS)
    step = norm / curve
    ratio = (image / curve) * step - 1.0
    step_out[...] = jnp.broadcast_to(step[:SIMS], (SIMS, NS))
    ratio_out[...] = jnp.broadcast_to(ratio[:SIMS], (SIMS, NS))
    drain()


def local(visibilities, transfer, noise_weight, freq_prior):
    vm = pl.BlockSpec(memory_space=pltpu.VMEM)
    hbm = pl.BlockSpec(memory_space=pltpu.HBM)
    dma = pltpu.SemaphoreType.DMA
    out = jax.ShapeDtypeStruct((NF, NM, SIMS, NS), F32)
    coef = jax.ShapeDtypeStruct((SIMS, NS), F32)
    slab = pltpu.VMEM((NFQ, OWN, LANES), BF16)
    wide = pltpu.VMEM((NFQ, OWN, LANES), F32)
    right, applied, step, ratio = pl.pallas_call(
        kernel,
        out_shape=(out, out, coef, coef),
        in_specs=[hbm] * 5,
        out_specs=(vm,) * 4,
        scratch_shapes=[
            pltpu.VMEM((NF, NM, NB, NS), BF16),
            pltpu.VMEM((NF, NM, NS, NB), BF16),
            pltpu.VMEM((256, 512), BF16),
            pltpu.VMEM((2, NY, TL, SIMS, HALF), BF16),
            pltpu.VMEM((32, 16, 128), BF16),
            pltpu.VMEM((16, 16, 128), BF16),
            pltpu.VMEM((15, 16, 128), BF16),
            pltpu.VMEM((NF, ROWS, NS), F32),
            pltpu.VMEM((NF, ROWS, NS), F32),
            slab, slab, slab, slab, wide, wide,
            pltpu.VMEM((NFQ, NF, F), F32),
            pltpu.VMEM((2, F * ROWS, F * ROWS), BF16),
            pltpu.VMEM((NF, NB), F32),
            pltpu.VMEM((2, 1, 128), F32),
            pltpu.VMEM((31, 1, 128), F32),
            pltpu.VMEM((7, 1, 128), F32),
            dma((NF,)), dma((5,)), dma((7,)), dma((7,)), dma((7,)), dma((7,)), dma((2,)), dma((2,)),
            dma((7,)), dma((7,)), dma((7,)), dma((7,)), dma((7,)), dma((7,)), dma, dma, dma, dma,
            pltpu.SemaphoreType.REGULAR((3,)),
        ],
        compiler_params=pltpu.CompilerParams(
            collective_id=0, has_side_effects=True, vmem_limit_bytes=40 * 1024 * 1024),
    )(*[pltpu.with_memory_space_constraint(v, pltpu.HBM) for v in
        (visibilities, transfer, noise_weight, freq_prior, jnp.asarray(cas_table()))])
    residual = right - step * applied
    return step * right, residual, residual + ratio * right


def solution(mesh):
    return jax.shard_map(
        local,
        mesh=mesh,
        in_specs=(
            P("ma", "freq", None, None),
            P("freq", "ma", None, None),
            P("freq", None),
            P("freq", None),
        ),
        out_specs=(P("freq", "ma", None, None),) * 3,
        check_vma=False,
    )
```

```python
import math

import jax
import jax.numpy as jnp
import numpy as np
from jax import lax
from jax.experimental import pallas as pl
from jax.experimental.pallas import tpu as pltpu
from jax.sharding import PartitionSpec as P

NZ, NY, NX, NC = 8, 4, 4, 2
NFQ = NX * NC
NF, NM, NB, NS, SIMS, NT, TL = 4, 2, 512, 1024, 4, 512, 16
F = NF * NFQ
ROWS = NM * SIMS
OWN = NF * ROWS
LANES = NS // NFQ
HALF = NB // 2
F32, BF16 = jnp.float32, jnp.bfloat16
HIGH = lax.Precision.HIGHEST
MA_GROUPS = [[(dz, dy) for dz in zs for dy in (2, 1, 3, 0) if dz or dy] for zs in ((3, 5, 1, 7), (4, 2, 6, 0))]
MA_OFFSETS = sorted(MA_GROUPS[0] + MA_GROUPS[1], key=lambda o: -min(o[0], NZ - o[0]) - min(o[1], NY - o[1]))
FQ_OFFSETS = [(dx, dc) for dx in range(NX) for dc in range(NC) if dx or dc]


def cas_table():
    m = np.arange(64)
    t = np.arange(NT)
    arg = (m[:, None] * t[None, :]) % NT
    ang = arg.astype(np.float32) * np.float32(2.0 * math.pi / NT)
    cas = (np.cos(ang) + np.sin(ang)) * np.float32(1.0 / math.sqrt(NT))
    cas = cas.reshape(64, NZ // 2, 128).transpose(1, 0, 2)
    eye = np.eye(SIMS, dtype=np.float32)
    full = cas[:, :, None, :, None] * eye[None, None, :, None, :]
    return full.reshape(NZ // 2, 256, 512).astype(jnp.bfloat16)


def dot(a, b, **kw):
    return jnp.dot(a, b, preferred_element_type=F32, **kw)


def dot_t(a, b):
    return lax.dot_general(a, b, (((1,), (1,)), ((), ())), preferred_element_type=F32)


def iota(shape, dim):
    return lax.broadcasted_iota(jnp.int32, shape, dim)


def lane_tiles(v):
    v = sum(v[i * ROWS:(i + 1) * ROWS] for i in range(NF))
    return sum(v[:, i * 128:(i + 1) * 128] for i in range(NS // 128))


def kernel(vis, transfer, weight_hbm, prior_hbm, cas, right_out, applied_out, step_out, ratio_out,
           tv, turned, casv, vbuf, pbuf, rbuf0, rbuf1, right, adj, rsl, rin, asl, ain, csl, cin, prior, spread, weight, dsend, d1, d2,
           tsem, lsem, ps, pr, a1s, a1r, a2s, a2r, rs, rr, as_, ar, cs, cr, d1s, d1r, d2s, d2r, round_sem):
    ma = lax.axis_index("ma")
    fq = lax.axis_index("freq")
    z, y = ma // NY, ma % NY
    rbuf = (rbuf0, rbuf1)
    x, c = fq // NC, fq % NC

    def ma_peer(dz, dy):
        return lax.rem(z + dz, NZ) * NY + lax.rem(y + dy, NY)

    def fq_peer(dx, dc):
        return lax.rem(x + dx, NX) * NC + lax.rem(c + dc, NC)

    def to_ma(dz, dy):
        return {"ma": ma_peer(dz, dy), "freq": fq}

    def to_fq(dx, dc):
        return {"ma": ma, "freq": fq_peer(dx, dc)}

    tcopies = [pltpu.make_async_copy(transfer.at[f], tv.at[f], tsem.at[f]) for f in range(NF)]
    odd = z % 2
    mate = z + 1 - 2 * odd
    other = lax.rem(z + NZ - 1 + 2 * odd, NZ)

    def half(h):
        return pl.ds(pl.multiple_of(h * HALF, HALF), HALF)

    cas_copy = pltpu.make_async_copy(cas.at[z // 2], casv, lsem.at[0])
    own_vis = [pltpu.make_async_copy(vis.at[:, y, :, half(odd)], vbuf.at[odd, y], lsem.at[1])]
    own_prior = pltpu.make_async_copy(prior_hbm, prior.at[fq], lsem.at[3])
    own_weight = pltpu.make_async_copy(weight_hbm, weight, lsem.at[4])
    local_copies = [*own_vis, cas_copy, own_prior, own_weight]

    def greet(sem, ma_offsets, fq_offsets):
        for o in ma_offsets:
            pl.semaphore_signal(sem, 1, device_id=to_ma(*o))
        for o in fq_offsets:
            pl.semaphore_signal(sem, 1, device_id=to_fq(*o))

    def at_z(zz, dy):
        return {"ma": zz * NY + lax.rem(y + dy, NY), "freq": fq}

    near = ([(1, 0), (NZ - 1, 0)], [(1, 0), (NX - 1, 0)])
    pair = [at_z(mate, dy) for dy in range(NY)] + [at_z(z, dy) for dy in range(1, NY)]
    barrier = pltpu.get_barrier_semaphore()
    for peer in pair + [at_z(other, 0)]:
        pl.semaphore_signal(barrier, 1, device_id=peer)
    greet(barrier, [], near[1] + [(0, 1)])
    for t in local_copies + tcopies:
        t.start()
    pl.semaphore_wait(barrier, len(pair) + 4)
    pending = []

    def send(src, dst, ssem, rsem, peer):
        copy = pltpu.make_async_remote_copy(src, dst, ssem, rsem, device_id=peer)
        copy.start()
        pending.append(copy)
        return copy

    def drain():
        for copy in pending:
            copy.wait_send()
        pending.clear()

    a1 = []
    for i, (peer, h, dy) in enumerate([(at_z(mate, 2), 1 - odd, 2), (at_z(z, 2), odd, 2), (at_z(mate, 1), 1 - odd, 1), (at_z(mate, 3), 1 - odd, 3),
                                              (at_z(z, 1), odd, 1), (at_z(z, 3), odd, 3), (at_z(mate, 0), 1 - odd, 0)]):
        a1.append(send(vis.at[:, lax.rem(y + dy, NY), :, half(h)], vbuf.at[odd, y], a1s.at[i], a1r.at[i], peer))
    greet(round_sem.at[0], *near)
    pl.semaphore_wait(round_sem.at[0], 4)
    greet(round_sem.at[1], [(2, 0), (NZ - 2, 0)], [(0, 1)])
    pl.semaphore_wait(round_sem.at[1], 3)
    greet(round_sem.at[2], near[0], [])
    pcs = [send(prior_hbm, prior.at[fq], ps.at[i], pr.at[i], to_fq(*o)) for i, o in enumerate(FQ_OFFSETS)]
    cas_copy.wait()
    pl.semaphore_wait(round_sem.at[2], 2)

    own_vis[0].wait()
    for r in a1:
        r.wait_recv()
    part = dot(casv[...], vbuf[...].reshape(512, HALF)).reshape(32, ROWS, HALF)
    pbuf[...] = jnp.concatenate([part[:, :, :128], part[:, :, 128:]], axis=1).astype(BF16)
    for h in range(2):
        for i, o in enumerate(MA_GROUPS[h]):
            pltpu.make_async_remote_copy(pbuf.at[ma_peer(*o)], rbuf[h].at[i], a2s.at[h], a2r.at[h], device_id=to_ma(*o)).start()

    own_prior.wait()
    own_weight.wait()
    for r in pcs:
        r.wait_recv()
    e1 = (iota((F * ROWS, F), 0) // ROWS == iota((F * ROWS, F), 1)).astype(F32)
    e2 = (iota((F, F * ROWS), 0) == iota((F, F * ROWS), 1) // ROWS).astype(F32)
    full = dot(dot(e1, prior[...].reshape(F, F), precision=HIGH), e2, precision=HIGH)
    same = iota((F * ROWS, F * ROWS), 0) % ROWS == iota((F * ROWS, F * ROWS), 1) % ROWS
    full = jnp.where(same, full, 0.0)
    spread[0] = full.astype(BF16)
    spread[1] = (full - full.astype(BF16).astype(F32)).astype(BF16)
    for t in tcopies:
        t.wait()

    @pl.loop(0, NF)
    def _(f):
        for m in range(NM):
            turned[f, m] = tv[f, m].T

    low = iota((ROWS, 1), 0) < SIMS

    def both(a, ref, f, at=slice(None)):
        return jnp.where(low, dot(a, ref[f, 0, at]), dot(a, ref[f, 1, at]))

    acc = [None] * NY
    for h in range(2):
        pltpu.make_async_copy(rbuf[h], rbuf[h], a2r.at[h]).wait()
        rows = half(1 - odd if h == 0 else odd)
        for dy in range(NY):
            f = lax.rem(y + NY - dy, NY)
            pieces = [rbuf[h][i] for i, o in enumerate(MA_GROUPS[h]) if o[1] == dy]
            if h == 1 and dy == 0:
                pieces.append(pbuf[ma])
            total = sum(p.astype(F32) for p in pieces)
            modes = jnp.concatenate([total[:ROWS], total[ROWS:]], axis=1)
            weighted = (weight[pl.ds(f, 1), rows] * modes).astype(BF16)
            out = both(weighted, tv, f, rows)
            acc[dy] = out if h == 0 else acc[dy] + out
    for dy in range(NY):
        right[lax.rem(y + NY - dy, NY)] = acc[dy]

    def slices(v, ref):
        v = v.astype(BF16)
        for j in range(NFQ):
            ref[j] = v[:, j * LANES:(j + 1) * LANES]

    rt = right[...].reshape(OWN, NS)
    slices(rt, rsl)
    rc = [send(rsl.at[fq_peer(*o)], rin.at[fq], rs.at[i], rr.at[i], to_fq(*o)) for i, o in enumerate(FQ_OFFSETS)]
    rin[fq] = rsl[fq]

    for dy in range(NY):
        f = lax.rem(y + NY - dy, NY)
        observed = both(acc[dy].astype(BF16), turned, f)
        scaled = (weight[pl.ds(f, 1), :] * observed).astype(BF16)
        adj[f] = both(scaled, tv, f)
    at = adj[...].reshape(OWN, NS)
    slices(at, asl)
    ac = [send(asl.at[fq_peer(*o)], ain.at[fq], as_.at[i], ar.at[i], to_fq(*o)) for i, o in enumerate(FQ_OFFSETS)]
    ain[fq] = asl[fq]

    for r in rc:
        r.wait_recv()
    rall = rin[...].reshape(F * ROWS, LANES)
    coupled = dot(spread[...].reshape(2 * F * ROWS, F * ROWS), rall)
    coupled = coupled[:F * ROWS] + coupled[F * ROWS:]

    def blocks(v):
        return sum(v[i * ROWS:(i + 1) * ROWS] for i in range(F))

    row, lane = iota((ROWS, 128), 0), iota((ROWS, 128), 1)

    def put(v, at_lane):
        return jnp.where(lane == row + at_lane, jnp.sum(v, axis=1, keepdims=True), 0.0)

    rest = put(lane_tiles(rt * rt), 0) + put(lane_tiles(rt * at) + blocks(rall.astype(F32) * coupled), ROWS)
    image = lane_tiles(at * at) + blocks(coupled * coupled)
    for r in ac:
        r.wait_recv()
    image = image + blocks(2.0 * ain[...].reshape(F * ROWS, LANES).astype(F32) * coupled)

    own = jnp.sum(rest + put(image, 2 * ROWS), axis=0, keepdims=True)
    dsend[0] = own
    for i, o in enumerate(FQ_OFFSETS):
        send(dsend.at[0], d2.at[i], d2s, d2r, to_fq(*o))
    for f in range(NF):
        for m in range(NM):
            right_out[f, m] = right[f, m * SIMS:(m + 1) * SIMS]
    for h in range(2):
        pltpu.make_async_copy(rbuf[h], rbuf[h], a2s.at[h]).wait()
    pltpu.make_async_copy(d2, d2, d2r).wait()
    own = own + jnp.sum(d2[...], axis=0)
    dsend[1] = own
    for i, o in enumerate(MA_OFFSETS):
        pltpu.make_async_remote_copy(dsend.at[1], d1.at[i], d1s, d1r, device_id=to_ma(*o)).start()
    csl[...] = coupled.reshape(NFQ, OWN, LANES)
    cc = [send(csl.at[fq_peer(*o)], cin.at[fq], cs.at[i], cr.at[i], to_fq(*o)) for i, o in enumerate(FQ_OFFSETS)]
    cin[fq] = csl[fq]
    for r in cc:
        r.wait_recv()
    for f in range(NF):
        coup = jnp.concatenate([cin[j, f * ROWS:(f + 1) * ROWS] for j in range(NFQ)], axis=1)
        applied = adj[f] + coup
        for m in range(NM):
            applied_out[f, m] = applied[m * SIMS:(m + 1) * SIMS]
    drain()
    pltpu.make_async_copy(d1, d1, d1s).wait()
    pltpu.make_async_copy(d1, d1, d1r).wait()
    own = own + jnp.sum(d1[...], axis=0)

    def take(at_lane):
        inside = (lane >= at_lane) & (lane < at_lane + ROWS) & (lane % SIMS == row % SIMS)
        return jnp.sum(jnp.where(inside, own, 0.0), axis=1, keepdims=True)

    norm, curve, image = take(0), take(ROWS), take(2 * ROWS)
    step = norm / curve
    ratio = (image / curve) * step - 1.0
    step_out[...] = jnp.broadcast_to(step[:SIMS], (SIMS, NS))
    ratio_out[...] = jnp.broadcast_to(ratio[:SIMS], (SIMS, NS))
    drain()


def local(visibilities, transfer, noise_weight, freq_prior):
    vm = pl.BlockSpec(memory_space=pltpu.VMEM)
    hbm = pl.BlockSpec(memory_space=pltpu.HBM)
    dma = pltpu.SemaphoreType.DMA
    out = jax.ShapeDtypeStruct((NF, NM, SIMS, NS), F32)
    coef = jax.ShapeDtypeStruct((SIMS, NS), F32)
    slab = pltpu.VMEM((NFQ, OWN, LANES), BF16)
    wide = pltpu.VMEM((NFQ, OWN, LANES), F32)
    right, applied, step, ratio = pl.pallas_call(
        kernel,
        out_shape=(out, out, coef, coef),
        in_specs=[hbm] * 5,
        out_specs=(vm,) * 4,
        scratch_shapes=[
            pltpu.VMEM((NF, NM, NB, NS), BF16),
            pltpu.VMEM((NF, NM, NS, NB), BF16),
            pltpu.VMEM((256, 512), BF16),
            pltpu.VMEM((2, NY, TL, SIMS, HALF), BF16),
            pltpu.VMEM((32, 16, 128), BF16),
            pltpu.VMEM((16, 16, 128), BF16),
            pltpu.VMEM((15, 16, 128), BF16),
            pltpu.VMEM((NF, ROWS, NS), F32),
            pltpu.VMEM((NF, ROWS, NS), F32),
            slab, slab, slab, slab, wide, wide,
            pltpu.VMEM((NFQ, NF, F), F32),
            pltpu.VMEM((2, F * ROWS, F * ROWS), BF16),
            pltpu.VMEM((NF, NB), F32),
            pltpu.VMEM((2, 1, 128), F32),
            pltpu.VMEM((31, 1, 128), F32),
            pltpu.VMEM((7, 1, 128), F32),
            dma((NF,)), dma((5,)), dma((7,)), dma((7,)), dma((7,)), dma((7,)), dma((2,)), dma((2,)),
            dma((7,)), dma((7,)), dma((7,)), dma((7,)), dma((7,)), dma((7,)), dma, dma, dma, dma,
            pltpu.SemaphoreType.REGULAR((3,)),
        ],
        compiler_params=pltpu.CompilerParams(
            collective_id=0, has_side_effects=True, vmem_limit_bytes=40 * 1024 * 1024),
    )(*[pltpu.with_memory_space_constraint(v, pltpu.HBM) for v in
        (visibilities, transfer, noise_weight, freq_prior, jnp.asarray(cas_table()))])
    residual = right - step * applied
    return step * right, residual, residual + ratio * right


def solution(mesh):
    return jax.shard_map(
        local,
        mesh=mesh,
        in_specs=(
            P("ma", "freq", None, None),
            P("freq", "ma", None, None),
            P("freq", None),
            P("freq", None),
        ),
        out_specs=(P("freq", "ma", None, None),) * 3,
        check_vma=False,
    )
```
